256 devices in a mesh: head: 4 (over z_lo), blk: 64 (over x, y, z_hi, core).
Axes of the slice: x: 4, y: 4, z: 8 (z_hi: 2, z_lo: 4; z = z_hi * 4 + z_lo), core: 2. Of those that a mesh axis runs over, the one named last changes fastest.
Arguments:
- queries: bfloat16 [64, 512, 4096], P('blk', 'head'), may hold values from -6 to 6
- key_rows: bfloat16 [64, 512, 512], P('blk', 'head'), may hold values from -6 to 6
- value_rows: bfloat16 [64, 512, 512], P('blk', 'head'), may hold values from -6 to 6
- attn_out: bfloat16 [64, 512, 4096], P('blk', 'head'), may hold values from -6 to 6
- out_grad: bfloat16 [64, 512, 4096], P('blk', 'head'), may hold values from -3 to 3
- log_norm: float32 [64, 512, 32], P('blk', 'head'), may hold values from 5 to 7
- block_layout: int32 [128], replicated, may hold values from 0 to 127, each once
Outputs:
- query_grad: bfloat16 [64, 512, 4096], P('blk', 'head')
- key_grad: bfloat16 [64, 512, 512], P('blk', 'head')
- value_grad: bfloat16 [64, 512, 512], P('blk', 'head')
The draws below stay inside these ranges and needn't reach their ends.
Inputs may be any that keep to these rules, and one draw needn't show every extreme that they name: Each block number stands once; the rows of blk index b are block block_layout[2 b] followed by block block_layout[2 b + 1].
All inputs are finite; a program needn't handle non-finite values.
Results may differ from the reference program's by a relative error of at most 0.014.
Values may be sent and summed in bfloat16 or wider, within the bound.
A program may use at most 128 MiB of HBM per device.

```python
import math
import jax
import jax.numpy as jnp
from jax import lax

HD = 128
KV_HEADS = 4
GROUP = 8
STEPS = 4
QH = 32
ROWS = 512
BLOCK = 256
BLOCKS = 128
N_BLK = 64


def levels(stream_key, extent, split, low, largest):
    loudness, own = 1.0, jax.random.fold_in(stream_key, 6)
    for dim, parts in split:
        heights = jnp.exp(jax.random.uniform(jax.random.fold_in(own, dim), (parts,), jnp.float32, low / len(split), largest / len(split)))
        loudness = loudness * jnp.repeat(heights, extent[dim] // parts).reshape([-1 if axis == dim else 1 for axis in range(len(extent))])
    return loudness


def bell_draw(rng, shape, scale, limit, split=(), kind=jnp.bfloat16):
    entries = scale * jax.random.normal(rng, shape, jnp.float32)
    if split:
        entries = entries * levels(rng, shape, split, -0.22, 0.18)
    return jnp.clip(entries, -limit, limit).astype(kind)


def setup_inputs(seed: int = 0) -> dict:
    seeds = jax.random.split(jax.random.key(seed), 8)
    queries = bell_draw(seeds[0], (N_BLK, ROWS, QH * HD), 1.0, 6.0, ((0, 64), (1, 4)))
    key_rows = bell_draw(seeds[1], (N_BLK, ROWS, KV_HEADS * HD), 1.0, 6.0, ((0, 64), (1, 4)))
    value_rows = bell_draw(seeds[2], (N_BLK, ROWS, KV_HEADS * HD), 1.0, 6.0, ((0, 64), (1, 4)))
    attn_out = bell_draw(seeds[3], (N_BLK, ROWS, QH * HD), 1.0, 6.0, ((0, 64), (1, 4)))
    out_grad = bell_draw(seeds[4], (N_BLK, ROWS, QH * HD), 0.5, 3.0, ((0, 64), (1, 4)))
    log_norm = jnp.clip(5.0 + 2.0 * jax.random.uniform(seeds[5], (N_BLK, ROWS, QH), jnp.float32) ** levels(seeds[5], (N_BLK, ROWS, QH), ((0, 64), (1, 4)), -0.2, 0.2), 5.0, 7.0)
    block_layout = jax.random.permutation(seeds[6], BLOCKS).astype(jnp.int32)
    return dict(queries=queries, key_rows=key_rows, value_rows=value_rows, attn_out=attn_out, out_grad=out_grad, log_norm=log_norm, block_layout=block_layout)


def tile_terms(query, dout, lse, delta, keys, vals, qpos, kpos, scale):
    f32 = jnp.float32
    scores = jnp.einsum('rkgd,ckd->kgrc', query.astype(f32), keys.astype(f32)) * scale
    linked = qpos[:, None] >= kpos[None, :]
    lse_t = jnp.transpose(lse, (1, 2, 0))
    delta_t = jnp.transpose(delta, (1, 2, 0))
    prob = jnp.where(linked[None, None], jnp.exp(scores - lse_t[..., None]), 0.0)
    prob16 = prob.astype(jnp.bfloat16)
    dprob = jnp.einsum('rkgd,ckd->kgrc', dout.astype(f32), vals.astype(f32))
    dscore = (prob * (dprob - delta_t[..., None])).astype(jnp.bfloat16)
    dval = jnp.einsum('kgrc,rkgd->ckd', prob16.astype(f32), dout.astype(f32))
    dkey = jnp.einsum('kgrc,rkgd->ckd', dscore.astype(f32), query.astype(f32))
    dquery = jnp.einsum('kgrc,ckd->rkgd', dscore.astype(f32), keys.astype(f32))
    return (dquery, dkey, dval)

def reference(queries, key_rows, value_rows, attn_out, out_grad, log_norm, block_layout):
    nblk, rows = (queries.shape[0], queries.shape[1])
    scale = 1.0 / math.sqrt(HD)
    qall = queries.reshape(nblk, rows, KV_HEADS, GROUP, HD)
    dall = out_grad.reshape(nblk, rows, KV_HEADS, GROUP, HD)
    oall = attn_out.reshape(nblk, rows, KV_HEADS, GROUP, HD)
    kall = key_rows.reshape(nblk, rows, KV_HEADS, HD)
    vall = value_rows.reshape(nblk, rows, KV_HEADS, HD)
    lall = log_norm.reshape(nblk, rows, KV_HEADS, GROUP)
    offsets = jnp.arange(rows, dtype=jnp.int32)
    within = offsets % BLOCK
    second = offsets // BLOCK

    def positions(owner):
        return jnp.take(block_layout, 2 * owner + second) * BLOCK + within

    def one_group(carry, index):
        dk_all, dv_all = carry
        query = qall[index]
        dout = dall[index]
        delta = lax.optimization_barrier(jnp.sum(dout.astype(jnp.float32) * oall[index].astype(jnp.float32), axis=-1))
        qpos = positions(index)
        dq_acc = jnp.zeros((rows, KV_HEADS, GROUP, HD), jnp.float32)
        for step in range(STEPS):
            owner = (index - step) % nblk
            dquery, dkey, dval = tile_terms(query, dout, lall[index], delta, kall[owner], vall[owner], qpos, positions(owner), scale)
            dq_acc = dq_acc + dquery
            dk_all = dk_all.at[owner].add(dkey)
            dv_all = dv_all.at[owner].add(dval)
        return ((dk_all, dv_all), dq_acc)
    start = (jnp.zeros((nblk, rows, KV_HEADS, HD), jnp.float32), jnp.zeros((nblk, rows, KV_HEADS, HD), jnp.float32))
    (dk_all, dv_all), dq_all = lax.scan(one_group, start, jnp.arange(nblk, dtype=jnp.int32))
    query_grad = (dq_all * scale).astype(jnp.bfloat16).reshape(nblk, rows, KV_HEADS * GROUP * HD)
    key_grad = (dk_all * scale).astype(jnp.bfloat16).reshape(nblk, rows, KV_HEADS * HD)
    value_grad = dv_all.astype(jnp.bfloat16).reshape(nblk, rows, KV_HEADS * HD)
    return (query_grad, key_grad, value_grad)
```

```python
import functools
import math

import jax
import jax.numpy as jnp
from jax import lax
from jax.experimental import pallas as pl
from jax.experimental.pallas import tpu as pltpu
from jax.sharding import PartitionSpec as P

HD = 128
GROUP = 8
KVH = 4
ROOT = math.sqrt(HD)
SCALE = 1.0 / ROOT
EXP2_SCALE = math.log2(math.e) / ROOT
BIG = 1e30
LINE = 4
MESH = pl.DeviceIdType.MESH
BF = jnp.bfloat16
F32 = jnp.float32


def nt(a, b):
    return lax.dot_general(a, b, (((1,), (1,)), ((), ())), preferred_element_type=F32)


def nn(a, b):
    return lax.dot_general(a, b, (((1,), (0,)), ((), ())), preferred_element_type=F32)


def tn(a, b):
    return lax.dot_general(a, b, (((0,), (0,)), ((), ())), preferred_element_type=F32)


def split3(x):
    hi = x.astype(BF).astype(F32)
    mid = (x - hi).astype(BF).astype(F32)
    return hi, mid, x - hi - mid


def kernel(
    n, layout, q_ref, k_hbm, v_hbm, o_ref, do_ref, lse_ref,
    dq_ref, dk_ref, dv_ref,
    lbuf, cbuf, sbuf, dbuf, aug, kcon, vcon, dq_t,
    part_l, part_c, out_s, out_d, out_c, out_l,
    in_s, in_d, in_c, in_x, in_r, in_w,
    sem_own, s_r, s_w, s_d, s_x, s_c, s_s, g_l, g_d, g_c, g_s,
    t_s, t_d, t_c, t_l, h_s, h_d, h_c, h_x, h_r, h_w,
):
    rows = q_ref.shape[1]
    b = lax.axis_index("blk")
    p = lax.axis_index("head")
    core = lax.rem(b, 2)

    def blk(i):
        return lax.rem(i + n, n)

    sib = b + 1 - 2 * core
    d_to = blk(b + 1 + 2 * core)
    d_from = blk(b - 3 + 2 * core)
    ahead = blk(b + 2)
    behind = blk(b - 2)

    def at(bb, pp):
        return {"blk": bb, "head": pp}

    def border(c, k):
        odd = lax.rem(k, 2)
        return jnp.where(odd == 1, (c + 3) // 2, c + c // 2)

    def both(*conds):
        out = conds[0]
        for c in conds[1:]:
            out = jnp.logical_and(out, c)
        return out

    def copy(src, dst, send, recv, dev):
        return pltpu.make_async_remote_copy(
            src_ref=src, dst_ref=dst, send_sem=send, recv_sem=recv,
            device_id=dev, device_id_type=MESH,
        )

    def c_right(k, u):
        return copy(lbuf.at[k, u], lbuf.at[k, u], s_r.at[k, u], g_l.at[k, u], at(b, p + 1))

    def c_left(k, u):
        return copy(lbuf.at[k, u], lbuf.at[k, u], s_w.at[k, u], g_l.at[k, u], at(b, p - 1))

    def c_d(k, u):
        return copy(lbuf.at[k, u], dbuf.at[k, u], s_d.at[k, u], g_d.at[k, u], at(d_to, p))

    def c_cross(k, u):
        return copy(lbuf.at[k, u], cbuf.at[k, u], s_x.at[k, u], g_c.at[k, u], at(ahead, 3 - p))

    def c_on(k, u, step):
        return copy(cbuf.at[k, u], cbuf.at[k, u], s_c.at[k, u], g_c.at[k, u], at(b, p + step))

    def c_sib(k, u):
        return copy(cbuf.at[k, u], sbuf.at[k, u], s_s.at[k, u], g_s.at[k, u], at(sib, p))

    def r_sib(k, u):
        return copy(out_s.at[k, u], in_s.at[k, u], t_s.at[k, u], h_s.at[k, u], at(sib, p))

    def r_d(k, u):
        return copy(out_d.at[k, u], in_d.at[k, u], t_d.at[k, u], h_d.at[k, u], at(d_from, p))

    def r_back(k, u, step):
        return copy(out_c.at[k, u], in_c.at[k, u], t_c.at[k, u], h_c.at[k, u], at(b, p + step))

    def r_cross(k, u):
        return copy(out_c.at[k, u], in_x.at[k, u], t_c.at[k, u], h_x.at[k, u], at(behind, 3 - p))

    def r_left(k, u):
        return copy(out_l.at[k, u], in_r.at[k, u], t_l.at[k, u], h_r.at[k, u], at(b, p - 1))

    def r_right(k, u):
        return copy(out_l.at[k, u], in_w.at[k, u], t_l.at[k, u], h_w.at[k, u], at(b, p + 1))

    def spread(k, u, act):
        pl.when(both(u <= p, p < LINE - 1))(lambda: act(c_right(k, u)))
        pl.when(both(u >= p, p > 0))(lambda: act(c_left(k, u)))
        over = jnp.logical_or(
            both(p == LINE - 1, u >= border(0, k)), both(p == 0, u < border(LINE - 1, k))
        )
        pl.when(over)(lambda: act(c_cross(k, u)))
        act(c_d(k, u))

    def pass_on(k, u, act):
        rising = u >= border(p, k)
        pl.when(both(rising, p < LINE - 1, u >= border(p + 1, k)))(lambda: act(c_on(k, u, 1)))
        pl.when(both(jnp.logical_not(rising), p > 0, u < border(p - 1, k)))(
            lambda: act(c_on(k, u, -1))
        )
        act(c_sib(k, u))

    start = lambda c: c.start()
    wait_send = lambda c: c.wait_send()

    def own_copy(k, part):
        src = (k_hbm, v_hbm)[part]
        lanes = pl.ds(pl.multiple_of(k * HD, HD), HD)
        return pltpu.make_async_copy(
            src.at[0, :, lanes], lbuf.at[k, p, part], sem_own.at[k, part]
        )

    def own_send(k):
        own_copy(k, 0).wait()
        own_copy(k, 1).wait()
        spread(k, p, start)

    def gather_gap(k, j):
        if j < LINE - 1:
            for u in (p - (j + 1), p + (j + 1)):
                @pl.when(both(u >= 0, u < LINE))
                def _(u=u):
                    c_right(k, u).wait_recv()
                    spread(k, u, start)
        up = 3 - (j - p)
        @pl.when(both(j >= p, up >= border(p, k)))
        def _():
            c_sib(k, up)
            c_on(k, up, 0).wait_recv()
            pass_on(k, up, start)
        down = j - (3 - p)
        @pl.when(both(down >= 0, down < border(p, k)))
        def _():
            c_on(k, down, 0).wait_recv()
            pass_on(k, down, start)

    def add(dst, src, k, u):
        dst[k, u] = dst[k, u] + src[k, u].astype(F32)

    def back_gap(k, j):
        def unit(u, rising):
            r_sib(k, u).wait_recv()
            add(part_c, in_s, k, u)
            if rising:
                more = both(p < LINE - 1, u >= border(p + 1, k))
            else:
                more = both(p > 0, u < border(p - 1, k))

            @pl.when(more)
            def _():
                r_back(k, u, 0).wait_recv()
                add(part_c, in_c, k, u)

            out_c[k, u] = part_c[k, u].astype(BF)
            send_back(k, u, rising, start)

        for u in range(LINE):
            pl.when(both(p == LINE - 1 - j, u >= border(p, k)))(lambda u=u: unit(u, True))
            pl.when(both(p == j, u < border(p, k)))(lambda u=u: unit(u, False))

    def send_back(k, u, rising, act):
        if rising:
            pl.when(p > 0)(lambda: act(r_back(k, u, -1)))
            pl.when(p == 0)(lambda: act(r_cross(k, u)))
        else:
            pl.when(p < LINE - 1)(lambda: act(r_back(k, u, 1)))
            pl.when(p == LINE - 1)(lambda: act(r_cross(k, u)))

    def sum_common(k, u):
        r_d(k, u).wait_recv()
        add(part_l, in_d, k, u)
        over = jnp.logical_or(
            both(p == LINE - 1, u >= border(0, k)), both(p == 0, u < border(LINE - 1, k))
        )

        @pl.when(over)
        def _():
            r_cross(k, u).wait_recv()
            add(part_l, in_x, k, u)

    def from_right(k, u):
        r_left(k, u).wait_recv()
        add(part_l, in_r, k, u)

    def from_left(k, u):
        r_right(k, u).wait_recv()
        add(part_l, in_w, k, u)

    def line_gap(k, j):
        def leftward(u):
            sum_common(k, u)
            pl.when(p < LINE - 1)(lambda: from_right(k, u))
            out_l[k, u] = part_l[k, u].astype(BF)
            r_left(k, u).start()

        def rightward(u):
            sum_common(k, u)
            pl.when(p > 0)(lambda: from_left(k, u))
            out_l[k, u] = part_l[k, u].astype(BF)
            r_right(k, u).start()

        for u in range(LINE):
            if j < LINE - 1:
                pl.when(both(p == LINE - 1 - j, u < p))(lambda u=u: leftward(u))
                pl.when(both(p == j, u > p))(lambda u=u: rightward(u))

    def finish(k):
        sum_common(k, p)
        pl.when(p < LINE - 1)(lambda: from_right(k, p))
        pl.when(p > 0)(lambda: from_left(k, p))
        lanes = pl.ds(pl.multiple_of(k * HD, HD), HD)
        dk_ref[0, :, lanes] = (part_l[k, p, 0] * SCALE).astype(BF)
        dv_ref[0, :, lanes] = part_l[k, p, 1].astype(BF)

    def prepare():
        lane = lax.broadcasted_iota(jnp.int32, (rows, HD), 1)

        def one(h, _):
            lanes = pl.ds(pl.multiple_of(h * HD, HD), HD)
            prod = do_ref[0, :, lanes].astype(F32) * o_ref[0, :, lanes].astype(F32)
            delta = jnp.sum(prod, axis=1, keepdims=True)
            which = lax.broadcasted_iota(jnp.int32, lse_ref.shape[1:], 1) == h
            lse = jnp.sum(jnp.where(which, lse_ref[0], 0.0), axis=1, keepdims=True) * ROOT
            w = jnp.where(lane == 3, 1.0, 0.0)
            for i, x in enumerate(split3(lse)):
                w = jnp.where(lane == i, x, w)
            for i, x in enumerate(split3(delta)):
                w = jnp.where(lane == 4 + i, x, w)
            aug[h] = w.astype(BF)
            return 0

        lax.fori_loop(0, KVH * GROUP, one, 0)
        vcon[...] = jnp.where(both(lane >= 4, lane < 7), -1.0, 0.0).astype(BF)
        mine = layout[2 * b + p // 2]
        for role, owner in enumerate((b, d_from, blk(sib - 2), behind)):
            for s in range(2):
                bias = jnp.where(layout[2 * owner + s] > mine, -BIG, 0.0)
                w = jnp.where(lane == 3, bias, jnp.where(lane < 3, -1.0, 0.0)).astype(BF)
                kcon[role, 2 * s] = w
                kcon[role, 2 * s + 1] = w

    keys_n = LINE * rows

    def chunk(k, role, buf):
        keys = buf[k, :, 0].reshape(keys_n, HD)
        vals = buf[k, :, 1].reshape(keys_n, HD)
        ka = jnp.concatenate([keys, kcon[role].reshape(keys_n, HD)], axis=1)
        va = jnp.concatenate([vals, jnp.concatenate([vcon[...]] * LINE, axis=0)], axis=1)
        qs, gs, qa, ga = [], [], [], []
        for g in range(GROUP):
            h = k * GROUP + g
            lanes = pl.ds(pl.multiple_of(h * HD, HD), HD)
            qs.append(q_ref[0, :, lanes])
            gs.append(do_ref[0, :, lanes])
            w = aug[h]
            qa.append(jnp.concatenate([qs[-1], w], axis=1))
            ga.append(jnp.concatenate([gs[-1], w], axis=1))
        qs, gs, qa, ga = [jnp.concatenate(x, axis=0) for x in (qs, gs, qa, ga)]
        st = nt(ka, qa)
        if role == 0:
            j = lax.broadcasted_iota(jnp.int32, st.shape, 0)
            t = lax.rem(lax.broadcasted_iota(jnp.int32, st.shape, 1), rows) + p * rows
            half = 2 * rows
            low = (p // 2) * half
            hidden = both(j > t, j >= low, j < low + half)
            st = jnp.where(hidden, -BIG, st)
        prob = jnp.exp2(st * EXP2_SCALE)
        ds = (prob * nt(va, ga)).astype(BF)
        dv = nn(prob.astype(BF), gs).reshape(LINE, rows, HD)
        dk = nn(ds, qs).reshape(LINE, rows, HD)
        dq = tn(keys, ds)
        if role == 0:
            dq_t[...] = dq
        else:
            dq_t[...] += dq
        return dk, dv

    def store(dst, k, dk, dv):
        dst[k, :, 0] = dk.astype(dst.dtype)
        dst[k, :, 1] = dv.astype(dst.dtype)

    def dq_out(k):
        for g in range(GROUP):
            lanes = pl.ds(pl.multiple_of((k * GROUP + g) * HD, HD), HD)
            tile = dq_t[:, g * rows:(g + 1) * rows] * SCALE
            dq_ref[0, :, lanes] = tile.T.astype(BF)

    for k in range(KVH):
        own_copy(k, 0).start()
        own_copy(k, 1).start()

    barrier = pltpu.get_barrier_semaphore()

    def greet(dev):
        pl.semaphore_signal(barrier, inc=1, device_id=dev, device_id_type=MESH)

    greet(at(sib, p))
    greet(at(blk(b + 3 - 6 * (1 - core)), p))
    pl.when(p > 0)(lambda: greet(at(b, p - 1)))
    pl.when(p < LINE - 1)(lambda: greet(at(b, p + 1)))
    at_end = jnp.logical_or(p == 0, p == LINE - 1)

    @pl.when(at_end)
    def _():
        greet(at(ahead, 3 - p))
        greet(at(behind, 3 - p))

    pl.semaphore_wait(barrier, jnp.where(at_end, 5, 4))

    own_send(0)
    prepare()
    own_send(1)
    for j in range(4):
        gather_gap(0, j)

    def gap(i, j):
        if isinstance(i, int):
            when = lambda cond, f: f() if cond else None
        else:
            when = lambda cond, f: pl.when(cond)(f)
        if j == 0:
            when(i < 2, lambda: own_send(i + 2))
        when(i < 3, lambda: gather_gap(i + 1, j))
        one = i >= 1 if not isinstance(i, int) else 1 <= i < 5
        two = i >= 2 if not isinstance(i, int) else 2 <= i < 6
        when(one, lambda: back_gap(i - 1, j))
        when(two, lambda: line_gap(i - 2, j))
        if j == 3:
            when(two, lambda: finish(i - 2))

    def head(k, _):
        gap(k, 0)
        dk, dv = chunk(k, 0, lbuf)
        store(part_l, k, dk, dv)
        gap(k, 1)
        for u in range(LINE):
            c_d(k, u).wait_recv()
        dk, dv = chunk(k, 1, dbuf)
        store(out_d, k, dk, dv)
        for u in range(LINE):
            r_d(k, u).start()
        gap(k, 2)
        for u in range(LINE):
            c_sib(k, u).wait_recv()
        dk, dv = chunk(k, 2, sbuf)
        store(out_s, k, dk, dv)
        for u in range(LINE):
            r_sib(k, u).start()
        gap(k, 3)
        dk, dv = chunk(k, 3, cbuf)
        store(part_c, k, dk, dv)
        dq_out(k)
        return 0

    lax.fori_loop(0, KVH, head, 0)
    for i in (4, 5):
        for j in range(4):
            gap(i, j)

    def drain(k, _):
        for u in range(LINE):
            spread(k, u, wait_send)
            pass_on(k, u, wait_send)
            r_d(k, u).wait_send()
            r_sib(k, u).wait_send()
            rising = u >= border(p, k)
            pl.when(rising)(lambda: send_back(k, u, True, wait_send))
            pl.when(jnp.logical_not(rising))(lambda: send_back(k, u, False, wait_send))
            pl.when(u < p)(lambda: r_left(k, u).wait_send())
            pl.when(u > p)(lambda: r_right(k, u).wait_send())
        return 0

    lax.fori_loop(0, KVH, drain, 0)


def solution(mesh):
    n = mesh.shape["blk"]
    vm = pl.BlockSpec(memory_space=pltpu.VMEM)
    anywhere = pl.BlockSpec(memory_space=pl.ANY)

    def shards(queries, key_rows, value_rows, attn_out, out_grad, log_norm, block_layout):
        rows = queries.shape[1]
        unit = (KVH, LINE, 2, rows, HD)
        sem = pltpu.SemaphoreType.DMA((KVH, LINE))
        return pl.pallas_call(
            functools.partial(kernel, n),
            out_shape=(
                jax.ShapeDtypeStruct(queries.shape, BF),
                jax.ShapeDtypeStruct(key_rows.shape, BF),
                jax.ShapeDtypeStruct(value_rows.shape, BF),
            ),
            in_specs=[
                pl.BlockSpec(memory_space=pltpu.SMEM), vm, anywhere, anywhere, vm, vm, vm,
            ],
            out_specs=(vm, vm, vm),
            scratch_shapes=[pltpu.VMEM(unit, BF)] * 4
            + [
                pltpu.VMEM((KVH * GROUP, rows, HD), BF),
                pltpu.VMEM((4, LINE, rows, HD), BF),
                pltpu.VMEM((rows, HD), BF),
                pltpu.VMEM((HD, GROUP * rows), F32),
            ]
            + [pltpu.VMEM(unit, F32)] * 2
            + [pltpu.VMEM(unit, BF)] * 4
            + [pltpu.VMEM(unit, BF)] * 6
            + [pltpu.SemaphoreType.DMA((KVH, 2))]
            + [sem] * 20,
            compiler_params=pltpu.CompilerParams(
                collective_id=0, has_side_effects=True, vmem_limit_bytes=56 * 2**20
            ),
        )(block_layout, queries, key_rows, value_rows, attn_out, out_grad, log_norm)

    placed = P("blk", "head", None)
    return jax.shard_map(
        shards,
        mesh=mesh,
        in_specs=(placed,) * 6 + (P(),),
        out_specs=(placed,) * 3,
        check_vma=False,
    )
```

```python
import functools
import math

import jax
import jax.numpy as jnp
from jax import lax
from jax.experimental import pallas as pl
from jax.experimental.pallas import tpu as pltpu
from jax.sharding import PartitionSpec as P

HD = 128
GROUP = 8
KVH = 4
ROOT = math.sqrt(HD)
SCALE = 1.0 / ROOT
EXP2_SCALE = math.log2(math.e) / ROOT
BIG = 1e30
LINE = 4
REACH = ((1, 2, 2, 3), (0, 1, 3, 4))
MESH = pl.DeviceIdType.MESH
BF = jnp.bfloat16
F32 = jnp.float32


def nt(a, b):
    return lax.dot_general(a, b, (((1,), (1,)), ((), ())), preferred_element_type=F32)


def nn(a, b):
    return lax.dot_general(a, b, (((1,), (0,)), ((), ())), preferred_element_type=F32)


def tn(a, b):
    return lax.dot_general(a, b, (((0,), (0,)), ((), ())), preferred_element_type=F32)


def split3(x):
    hi = x.astype(BF).astype(F32)
    mid = (x - hi).astype(BF).astype(F32)
    return hi, mid, x - hi - mid


def kernel(
    n, layout, q_ref, k_hbm, v_hbm, o_ref, do_ref, lse_ref,
    dq_ref, dk_ref, dv_ref,
    got, aug, kcon, vcon, dq_t, part, acc, out_c, out_l,
    in_s, in_d, in_c, in_x, in_r, in_w,
    sem_own, s_r, s_w, s_x, s_c, s_d, s_s, g_l, g_c, g_d, g_s,
    t_c, t_l, t_s, t_d, h_c, h_x, h_r, h_w, h_s, h_d,
):
    rows = q_ref.shape[1]
    b = lax.axis_index("blk")
    p = lax.axis_index("head")
    core = lax.rem(b, 2)
    lbuf, dbuf, sbuf, cbuf = [got.at[role] for role in range(4)]

    def blk(i):
        return lax.rem(i + n, n)

    sib = b + 1 - 2 * core
    d_to = blk(b + 1 + 2 * core)
    d_from = blk(b - 3 + 2 * core)
    ahead = blk(b + 2)
    behind = blk(b - 2)

    def at(bb, pp):
        return {"blk": bb, "head": pp}

    def both(*conds):
        out = conds[0]
        for c in conds[1:]:
            out = jnp.logical_and(out, c)
        return out

    def reach(u, k):
        if isinstance(k, int):
            return REACH[k % 2][u]
        return jnp.where(lax.rem(k, 2) == 1, REACH[1][u], REACH[0][u])

    def copy(src, dst, send, recv, dev):
        return pltpu.make_async_remote_copy(
            src_ref=src, dst_ref=dst, send_sem=send, recv_sem=recv,
            device_id=dev, device_id_type=MESH,
        )

    def c_right(k, u):
        return copy(lbuf.at[k, u], lbuf.at[k, u], s_r.at[k, u], g_l.at[k, u], at(b, p + 1))

    def c_left(k, u):
        return copy(lbuf.at[k, u], lbuf.at[k, u], s_w.at[k, u], g_l.at[k, u], at(b, p - 1))

    def c_cross(k, u):
        return copy(lbuf.at[k, u], cbuf.at[k, u], s_x.at[k, u], g_c.at[k, u], at(ahead, 3 - p))

    def c_on(k, u, step):
        return copy(cbuf.at[k, u], cbuf.at[k, u], s_c.at[k, u], g_c.at[k, u], at(b, p + step))

    def c_d(k, u):
        return copy(lbuf.at[k, u], dbuf.at[k, u], s_d.at[k], g_d.at[k], at(d_to, p))

    def c_sib(k, u):
        return copy(cbuf.at[k, u], sbuf.at[k, u], s_s.at[k], g_s.at[k], at(sib, p))

    def c_d_all(k):
        return copy(lbuf.at[k], dbuf.at[k], s_d.at[k], g_d.at[k], at(d_to, p))

    def c_sib_all(k):
        return copy(cbuf.at[k], sbuf.at[k], s_s.at[k], g_s.at[k], at(sib, p))

    def r_sib(k):
        return copy(part.at[2, k], in_s.at[k], t_s.at[k], h_s.at[k], at(sib, p))

    def r_d(k):
        return copy(part.at[1, k], in_d.at[k], t_d.at[k], h_d.at[k], at(d_from, p))

    def r_back(k, u, step):
        return copy(out_c.at[k, u], in_c.at[k, u], t_c.at[k, u], h_c.at[k, u], at(b, p + step))

    def r_cross(k, u):
        return copy(out_c.at[k, u], in_x.at[k, u], t_c.at[k, u], h_x.at[k, u], at(behind, 3 - p))

    def r_left(k, u):
        return copy(out_l.at[k, u], in_r.at[k, u], t_l.at[k, u], h_r.at[k, u], at(b, p - 1))

    def r_right(k, u):
        return copy(out_l.at[k, u], in_w.at[k, u], t_l.at[k, u], h_w.at[k, u], at(b, p + 1))

    start = lambda c: c.start()
    wait_send = lambda c: c.wait_send()

    def crosses(k, u):
        return jnp.logical_or(
            both(p == LINE - 1, reach(u, k) > 0), both(p == 0, reach(u, k) < LINE)
        )

    def spread(k, u, act):
        pl.when(crosses(k, u))(lambda: act(c_cross(k, u)))
        pl.when(both(u <= p, p < LINE - 1))(lambda: act(c_right(k, u)))
        pl.when(both(u >= p, p > 0))(lambda: act(c_left(k, u)))

    def pass_on(k, u, act):
        top = reach(u, k)
        pl.when(p + 1 < top)(lambda: act(c_on(k, u, 1)))
        pl.when(p > top)(lambda: act(c_on(k, u, -1)))

    def own_copy(k, which):
        src = (k_hbm, v_hbm)[which]
        lanes = pl.ds(pl.multiple_of(k * HD, HD), HD)
        return pltpu.make_async_copy(
            src.at[0, :, lanes], lbuf.at[k, p, which], sem_own.at[k, which]
        )

    def own_send(k):
        own_copy(k, 0).wait()
        own_copy(k, 1).wait()
        for u in range(LINE):
            @pl.when(p == u)
            def _(u=u):
                spread(k, u, start)
                c_d(k, u).start()

    def gather(k, j):
        for u in range(LINE):
            if j < LINE - 1:
                @pl.when(jnp.logical_or(p - u == j + 1, u - p == j + 1))
                def _(u=u):
                    c_right(k, u).wait_recv()
                    spread(k, u, start)
                    c_d(k, u).start()

            top = reach(u, k)
            rise = both(p < top, p + (3 - u) == j)
            fall = both(p >= top, u + 3 - p == j)

            @pl.when(jnp.logical_or(rise, fall))
            def _(u=u):
                c_cross(k, u).wait_recv()
                pass_on(k, u, start)
                c_sib(k, u).start()

    def add(src, k, u):
        acc[...] += src[k, u].astype(F32)

    def send_back(k, u, act):
        top = reach(u, k)
        pl.when(both(p < top, p > 0))(lambda: act(r_back(k, u, -1)))
        pl.when(both(p >= top, p < LINE - 1))(lambda: act(r_back(k, u, 1)))
        pl.when(jnp.logical_or(both(p < top, p == 0), both(p >= top, p == LINE - 1)))(
            lambda: act(r_cross(k, u))
        )

    def line_terms(k, u):
        acc[...] = part[0, k, u].astype(F32)
        add(in_d, k, u)

        @pl.when(crosses(k, u))
        def _():
            r_cross(k, u).wait_recv()
            add(in_x, k, u)

    def from_right(k, u):
        r_left(k, u).wait_recv()
        add(in_r, k, u)

    def from_left(k, u):
        r_right(k, u).wait_recv()
        add(in_w, k, u)

    def finish(k, u):
        line_terms(k, u)
        pl.when(p < LINE - 1)(lambda: from_right(k, u))
        pl.when(p > 0)(lambda: from_left(k, u))
        lanes = pl.ds(pl.multiple_of(k * HD, HD), HD)
        dk_ref[0, :, lanes] = (acc[0] * SCALE).astype(BF)
        dv_ref[0, :, lanes] = acc[1].astype(BF)

    def back(k, t):
        if t == 0:
            r_sib(k).wait_recv()
        if t == 1:
            r_d(k).wait_recv()
        for u in range(LINE):
            top = reach(u, k)
            if t < LINE:
                last = jnp.logical_or(p == top - 1, p == top) if t == 0 else None
                turn = last if t == 0 else jnp.logical_or(p == top - 1 - t, p == top + t)

                @pl.when(turn)
                def _(u=u):
                    acc[...] = part[3, k, u].astype(F32)
                    add(in_s, k, u)
                    if t > 0:
                        r_back(k, u, 0).wait_recv()
                        add(in_c, k, u)
                    out_c[k, u] = acc[...].astype(BF)
                    send_back(k, u, start)

            if t > 0:
                @pl.when(both(p > u, jnp.maximum(1, top) + 3 - p == t))
                def _(u=u):
                    line_terms(k, u)
                    pl.when(p < LINE - 1)(lambda: from_right(k, u))
                    out_l[k, u] = acc[...].astype(BF)
                    r_left(k, u).start()

                @pl.when(both(p < u, jnp.maximum(1, LINE - top) + p == t))
                def _(u=u):
                    line_terms(k, u)
                    pl.when(p > 0)(lambda: from_left(k, u))
                    out_l[k, u] = acc[...].astype(BF)
                    r_right(k, u).start()

            if t == LINE:
                pl.when(p == u)(lambda u=u: finish(k, u))

    def prepare():
        lane = lax.broadcasted_iota(jnp.int32, (rows, HD), 1)
        lses = lse_ref[0].T * ROOT
        heads = lax.broadcasted_iota(jnp.int32, lses.shape, 1)

        def one(h, _):
            lanes = pl.ds(pl.multiple_of(h * HD, HD), HD)
            prod = do_ref[0, :, lanes].astype(F32) * o_ref[0, :, lanes].astype(F32)
            delta = jnp.sum(prod, axis=1, keepdims=True)
            lse = jnp.sum(jnp.where(heads == h, lses, 0.0), axis=1, keepdims=True)
            w = jnp.where(lane == 3, 1.0, 0.0)
            for i, x in enumerate(split3(lse)):
                w = jnp.where(lane == i, x, w)
            for i, x in enumerate(split3(delta)):
                w = jnp.where(lane == 4 + i, x, w)
            aug[h] = w.astype(BF)
            return 0

        lax.fori_loop(0, KVH * GROUP, one, 0)
        vcon[...] = jnp.where(both(lane >= 4, lane < 7), -1.0, 0.0).astype(BF)
        dq_t[...] = jnp.zeros_like(dq_t)
        mine = layout[2 * b + p // 2]
        for role, owner in enumerate((b, d_from, blk(sib - 2), behind)):
            for s in range(2):
                bias = jnp.where(layout[2 * owner + s] > mine, -BIG, 0.0)
                w = jnp.where(lane == 3, bias, jnp.where(lane < 3, -1.0, 0.0)).astype(BF)
                kcon[role, 2 * s] = w
                kcon[role, 2 * s + 1] = w

    keys_n = LINE * rows

    def chunk(k, role, own):
        keys = got[role, k, :, 0].reshape(keys_n, HD)
        vals = got[role, k, :, 1].reshape(keys_n, HD)
        ka = jnp.concatenate([keys, kcon[role].reshape(keys_n, HD)], axis=1)
        va = jnp.concatenate([vals, jnp.concatenate([vcon[...]] * LINE, axis=0)], axis=1)
        qs, gs, qa, ga = [], [], [], []
        for g in range(GROUP):
            h = k * GROUP + g
            lanes = pl.ds(pl.multiple_of(h * HD, HD), HD)
            qs.append(q_ref[0, :, lanes])
            gs.append(do_ref[0, :, lanes])
            w = aug[h]
            qa.append(jnp.concatenate([qs[-1], w], axis=1))
            ga.append(jnp.concatenate([gs[-1], w], axis=1))
        qs, gs, qa, ga = [jnp.concatenate(x, axis=0) for x in (qs, gs, qa, ga)]
        st = nt(ka, qa)
        if own:
            j = lax.broadcasted_iota(jnp.int32, st.shape, 0)
            t = lax.rem(lax.broadcasted_iota(jnp.int32, st.shape, 1), rows) + p * rows
            half = 2 * rows
            low = (p // 2) * half
            hidden = both(j > t, j >= low, j < low + half)
            st = jnp.where(hidden, -BIG, st)
        prob = jnp.exp2(st * EXP2_SCALE)
        ds = (prob * nt(va, ga)).astype(BF)
        part[role, k, :, 1] = nn(prob.astype(BF), gs).reshape(LINE, rows, HD).astype(BF)
        part[role, k, :, 0] = nn(ds, qs).reshape(LINE, rows, HD).astype(BF)
        dq_t[...] += tn(keys, ds)

    def dq_out(k):
        for g in range(GROUP):
            lanes = pl.ds(pl.multiple_of((k * GROUP + g) * HD, HD), HD)
            tile = dq_t[:, g * rows:(g + 1) * rows] * SCALE
            dq_ref[0, :, lanes] = tile.T.astype(BF)
        dq_t[...] = jnp.zeros_like(dq_t)

    for k in range(KVH):
        own_copy(k, 0).start()
        own_copy(k, 1).start()

    barrier = pltpu.get_barrier_semaphore()

    def greet(dev):
        pl.semaphore_signal(barrier, inc=1, device_id=dev, device_id_type=MESH)

    greet(at(sib, p))
    greet(at(blk(b + 3 - 6 * (1 - core)), p))
    pl.when(p > 0)(lambda: greet(at(b, p - 1)))
    pl.when(p < LINE - 1)(lambda: greet(at(b, p + 1)))
    at_end = jnp.logical_or(p == 0, p == LINE - 1)

    @pl.when(at_end)
    def _():
        greet(at(ahead, 3 - p))
        greet(at(behind, 3 - p))

    pl.semaphore_wait(barrier, jnp.where(at_end, 5, 4))

    own_send(0)
    prepare()
    gather(0, 0)
    own_send(1)
    gather(0, 1)
    gather(1, 0)
    gather(0, 2)

    def when(cond, f):
        pl.when(cond)(f)

    def step(c, _):
        i = lax.div(c, 4)
        s = lax.rem(c, 4)

        @pl.when(s == 0)
        def _():
            when(i < 3, lambda: gather(i + 1, 1))
            when(i == 1, lambda: back(0, 0))

        @pl.when(s == 1)
        def _():
            when(i == 0, lambda: gather(0, 3))
            when(i < 3, lambda: gather(i + 1, 2))
            when(i < 2, lambda: own_send(i + 2))
            when(i >= 1, lambda: back(i - 1, 1))
            when(i >= 2, lambda: back(i - 2, 3))

        @pl.when(s == 3)
        def _():
            when(i < 3, lambda: gather(i + 1, 3))
            when(i < 2, lambda: gather(i + 2, 0))
            when(i >= 1, lambda: back(i, 0))
            when(i >= 1, lambda: back(i - 1, 2))
            when(i >= 2, lambda: back(i - 2, 4))

        role = jnp.where(i == 0, s, jnp.where(s < 2, s + 2, 3 - s))
        when(role == 1, lambda: c_d_all(i).wait_recv())
        when(role == 2, lambda: c_sib_all(i).wait_recv())
        when(role == 0, lambda: chunk(i, 0, True))
        when(role > 0, lambda: chunk(i, role, False))
        when(role == 1, lambda: r_d(i).start())
        when(role == 2, lambda: r_sib(i).start())
        when(s == 3, lambda: dq_out(i))
        return 0

    lax.fori_loop(0, 4 * KVH, step, 0)
    back(3, 1)
    back(2, 3)
    back(3, 2)
    back(2, 4)
    back(3, 3)
    back(3, 4)

    def drain(k, _):
        for u in range(LINE):
            spread(k, u, wait_send)
            pass_on(k, u, wait_send)
            send_back(k, u, wait_send)
            pl.when(u < p)(lambda: r_left(k, u).wait_send())
            pl.when(u > p)(lambda: r_right(k, u).wait_send())
        c_d_all(k).wait_send()
        c_sib_all(k).wait_send()
        r_d(k).wait_send()
        r_sib(k).wait_send()
        return 0

    lax.fori_loop(0, KVH, drain, 0)


def solution(mesh):
    n = mesh.shape["blk"]
    vm = pl.BlockSpec(memory_space=pltpu.VMEM)
    anywhere = pl.BlockSpec(memory_space=pl.ANY)

    def shards(queries, key_rows, value_rows, attn_out, out_grad, log_norm, block_layout):
        rows = queries.shape[1]
        unit = (KVH, LINE, 2, rows, HD)
        sem = pltpu.SemaphoreType.DMA((KVH, LINE))
        sems = pltpu.SemaphoreType.DMA((KVH,))
        log_norm = jnp.transpose(log_norm, (0, 2, 1))
        return pl.pallas_call(
            functools.partial(kernel, n),
            out_shape=(
                jax.ShapeDtypeStruct(queries.shape, BF),
                jax.ShapeDtypeStruct(key_rows.shape, BF),
                jax.ShapeDtypeStruct(value_rows.shape, BF),
            ),
            in_specs=[
                pl.BlockSpec(memory_space=pltpu.SMEM), vm, anywhere, anywhere, vm, vm, vm,
            ],
            out_specs=(vm, vm, vm),
            scratch_shapes=[
                pltpu.VMEM((4,) + unit, BF),
                pltpu.VMEM((KVH * GROUP, rows, HD), BF),
                pltpu.VMEM((4, LINE, rows, HD), BF),
                pltpu.VMEM((rows, HD), BF),
                pltpu.VMEM((HD, GROUP * rows), F32),
                pltpu.VMEM((4,) + unit, BF),
                pltpu.VMEM((2, rows, HD), F32),
            ]
            + [pltpu.VMEM(unit, BF)] * 8
            + [pltpu.SemaphoreType.DMA((KVH, 2))]
            + [sem] * 4 + [sems] * 2 + [sem] * 2 + [sems] * 2
            + [sem] * 2 + [sems] * 2 + [sem] * 4 + [sems] * 2,
            compiler_params=pltpu.CompilerParams(
                collective_id=0, has_side_effects=True, vmem_limit_bytes=56 * 2**20
            ),
        )(block_layout, queries, key_rows, value_rows, attn_out, out_grad, log_norm)

    placed = P("blk", "head", None)
    return jax.shard_map(
        shards,
        mesh=mesh,
        in_specs=(placed,) * 6 + (P(),),
        out_specs=(placed,) * 3,
        check_vma=False,
    )
```

```python
import functools
import math

import jax
import jax.numpy as jnp
from jax import lax
from jax.experimental import pallas as pl
from jax.experimental.pallas import tpu as pltpu
from jax.sharding import PartitionSpec as P

HD = 128
GROUP = 8
KVH = 4
ROOT = math.sqrt(HD)
SCALE = 1.0 / ROOT
EXP2_SCALE = math.log2(math.e) / ROOT
BIG = 1e30
LINE = 4
REACH = (0, 1, 3, 4)
REACH_LAST = (1, 2, 2, 3)
LAST = KVH - 1
MESH = pl.DeviceIdType.MESH
BF = jnp.bfloat16
F32 = jnp.float32


def nt(a, b):
    return lax.dot_general(a, b, (((1,), (1,)), ((), ())), preferred_element_type=F32)


def nn(a, b):
    return lax.dot_general(a, b, (((1,), (0,)), ((), ())), preferred_element_type=F32)


def tn(a, b):
    return lax.dot_general(a, b, (((0,), (0,)), ((), ())), preferred_element_type=F32)


def split3(x):
    hi = x.astype(BF).astype(F32)
    mid = (x - hi).astype(BF).astype(F32)
    return hi, mid, x - hi - mid


def kernel(
    n, layout, q_hbm, k_hbm, v_hbm, o_hbm, do_hbm, lse_ref,
    dq_hbm, dk_ref, dv_ref,
    q_ref, o_ref, do_ref, dq_ref, sem_in, sem_out, got, aug, kcon, vcon, kept, part, acc, out_c, out_l,
    in_s, in_d, in_c, in_x, in_r, in_w, in_u,
    sem_own, s_r, s_w, s_x, s_c, s_d, s_s, g_l, g_c, g_d, g_s,
    t_c, t_l, t_s, t_d, h_c, h_x, h_r, h_w, h_s, h_d, h_u,
):
    rows = q_ref.shape[0]
    b = lax.axis_index("blk")
    p = lax.axis_index("head")
    core = lax.rem(b, 2)
    lbuf, dbuf, sbuf, cbuf = [got.at[role] for role in range(4)]

    def blk(i):
        return lax.rem(i + n, n)

    sib = b + 1 - 2 * core
    d_to = blk(b + 1 + 2 * core)
    d_from = blk(b - 3 + 2 * core)
    ahead = blk(b + 2)
    behind = blk(b - 2)

    def at(bb, pp):
        return {"blk": bb, "head": pp}

    def both(*conds):
        out = conds[0]
        for c in conds[1:]:
            out = jnp.logical_and(out, c)
        return out

    def reach(u, k):
        if isinstance(k, int):
            return REACH_LAST[u] if k % 2 == 1 else REACH[u]
        return jnp.where(lax.rem(k, 2) == 1, REACH_LAST[u], REACH[u])

    def copy(src, dst, send, recv, dev):
        return pltpu.make_async_remote_copy(
            src_ref=src, dst_ref=dst, send_sem=send, recv_sem=recv,
            device_id=dev, device_id_type=MESH,
        )

    def c_right(k, u):
        return copy(lbuf.at[k, u], lbuf.at[k, u], s_r.at[k, u], g_l.at[k, u], at(b, p + 1))

    def c_left(k, u):
        return copy(lbuf.at[k, u], lbuf.at[k, u], s_w.at[k, u], g_l.at[k, u], at(b, p - 1))

    def c_cross(k, u):
        return copy(lbuf.at[k, u], cbuf.at[k, u], s_x.at[k, u], g_c.at[k, u], at(ahead, 3 - p))

    def c_on(k, u, step):
        return copy(cbuf.at[k, u], cbuf.at[k, u], s_c.at[k, u], g_c.at[k, u], at(b, p + step))

    def c_sib(k, u):
        return copy(cbuf.at[k, u], sbuf.at[k, u], s_s.at[k], g_s.at[k], at(sib, p))

    def c_d_all(k):
        return copy(lbuf.at[k], dbuf.at[k], s_d.at[k], g_d.at[k], at(d_to, p))

    def c_sib_all(k):
        return copy(cbuf.at[k], sbuf.at[k], s_s.at[k], g_s.at[k], at(sib, p))

    def r_sib(k):
        return copy(part.at[2, k], in_s.at[k], t_s.at[k], h_s.at[k], at(sib, p))

    def r_d(k):
        return copy(part.at[1, k], in_d.at[k], t_d.at[k], h_d.at[k], at(d_from, p))

    def r_back(k, u, step):
        return copy(out_c.at[k, u], in_c.at[k, u], t_c.at[k, u], h_c.at[k, u], at(b, p + step))

    def r_cross(k, u):
        return copy(out_c.at[k, u], in_x.at[k, u], t_c.at[k, u], h_x.at[k, u], at(behind, 3 - p))

    def r_left(k, u):
        return copy(out_l.at[k, u], in_r.at[k, u], t_l.at[k, u], h_r.at[k, u], at(b, p - 1))

    def r_right(k, u):
        return copy(out_l.at[k, u], in_w.at[k, u], t_l.at[k, u], h_w.at[k, u], at(b, p + 1))

    def r_owner(u, place):
        return copy(out_l.at[LAST, u], in_u.at[place], t_l.at[LAST, u], h_u.at[place], at(b, u))

    start = lambda c: c.start()
    wait_send = lambda c: c.wait_send()

    def crosses(k, u):
        return jnp.logical_or(
            both(p == LINE - 1, reach(u, k) > 0), both(p == 0, reach(u, k) < LINE)
        )

    def spread(k, u, act):
        pl.when(crosses(k, u))(lambda: act(c_cross(k, u)))
        pl.when(both(u <= p, p < LINE - 1))(lambda: act(c_right(k, u)))
        pl.when(both(u >= p, p > 0))(lambda: act(c_left(k, u)))

    def pass_on(k, u, act):
        top = reach(u, k)
        pl.when(p + 1 < top)(lambda: act(c_on(k, u, 1)))
        pl.when(p > top)(lambda: act(c_on(k, u, -1)))

    def own_copy(k, which):
        src = (k_hbm, v_hbm)[which]
        lanes = pl.ds(pl.multiple_of(k * HD, HD), HD)
        return pltpu.make_async_copy(
            src.at[0, :, lanes], lbuf.at[k, p, which], sem_own.at[k, which]
        )

    def own_send(k):
        own_copy(k, 0).wait()
        own_copy(k, 1).wait()
        for u in range(LINE):
            @pl.when(p == u)
            def _(u=u):
                spread(k, u, start)

    def gather(k, j):
        for u in range(LINE):
            if j < LINE - 1:
                @pl.when(jnp.logical_or(p - u == j + 1, u - p == j + 1))
                def _(u=u):
                    c_right(k, u).wait_recv()
                    spread(k, u, start)

            top = reach(u, k)
            rise = both(p < top, p + (3 - u) == j)
            fall = both(p >= top, u + 3 - p == j)

            @pl.when(jnp.logical_or(rise, fall))
            def _(u=u):
                c_cross(k, u).wait_recv()
                pass_on(k, u, start)
                c_sib(k, u).start()

    def add(src, k, u):
        acc[...] += src[k, u].astype(F32)

    def send_back(k, u, act):
        top = reach(u, k)
        pl.when(both(p < top, p > 0))(lambda: act(r_back(k, u, -1)))
        pl.when(both(p >= top, p < LINE - 1))(lambda: act(r_back(k, u, 1)))
        pl.when(jnp.logical_or(both(p < top, p == 0), both(p >= top, p == LINE - 1)))(
            lambda: act(r_cross(k, u))
        )

    def line_terms(k, u):
        acc[...] = part[0, k, u].astype(F32)
        add(in_d, k, u)

        @pl.when(crosses(k, u))
        def _():
            r_cross(k, u).wait_recv()
            add(in_x, k, u)

    def from_right(k, u):
        r_left(k, u).wait_recv()
        add(in_r, k, u)

    def from_left(k, u):
        r_right(k, u).wait_recv()
        add(in_w, k, u)

    def finish(k, u):
        line_terms(k, u)
        pl.when(p < LINE - 1)(lambda: from_right(k, u))
        pl.when(p > 0)(lambda: from_left(k, u))
        write_out(k)

    def write_out(k):
        lanes = pl.ds(pl.multiple_of(k * HD, HD), HD)
        dk_ref[0, :, lanes] = (acc[0] * (2 * SCALE)).astype(BF)
        dv_ref[0, :, lanes] = (acc[1] * 2.0).astype(BF)

    def line_ahead(k, t):
        for u in range(LINE):
            top = reach(u, k)

            @pl.when(jnp.logical_or(p == top - 1 - t, p == top + t))
            def _(u=u):
                acc[...] = part[3, k, u].astype(F32)
                add(in_s, k, u)
                if t > 0:
                    r_back(k, u, 0).wait_recv()
                    add(in_c, k, u)
                out_c[k, u] = acc[...].astype(BF)
                send_back(k, u, start)

    def back(k, t):
        if t == 0:
            r_sib(k).wait_recv()
        if t == 1:
            r_d(k).wait_recv()
        if t < LINE:
            line_ahead(k, t)
        for u in range(LINE):
            top = reach(u, k)
            if t > 0:
                @pl.when(both(p > u, jnp.maximum(1, top) + 3 - p == t))
                def _(u=u):
                    line_terms(k, u)
                    pl.when(p < LINE - 1)(lambda: from_right(k, u))
                    out_l[k, u] = acc[...].astype(BF)
                    r_left(k, u).start()

                @pl.when(both(p < u, jnp.maximum(1, LINE - top) + p == t))
                def _(u=u):
                    line_terms(k, u)
                    pl.when(p > 0)(lambda: from_left(k, u))
                    out_l[k, u] = acc[...].astype(BF)
                    r_right(k, u).start()

            if t == LINE:
                pl.when(p == u)(lambda u=u: finish(k, u))

    def back_last(t):
        if t == 1:
            r_d(LAST).wait_recv()
        if t < LINE - 1:
            line_ahead(LAST, t)
        for u in range(LINE):
            top = REACH_LAST[u]
            turn = jnp.where(p == LINE - 1, max(1, top), jnp.where(p == 0, max(1, LINE - top), 1))

            @pl.when(both(p != u, turn == t))
            def _(u=u):
                line_terms(LAST, u)
                out_l[LAST, u] = acc[...].astype(BF)
                r_owner(u, p).start()

        if t == LINE - 1:
            for u in range(LINE):
                @pl.when(p == u)
                def _(u=u):
                    line_terms(LAST, u)
                    for place in range(LINE):
                        if place != u:
                            r_owner((u + 1) % LINE, place).wait_recv()
                            acc[...] += in_u[place].astype(F32)
                    write_out(LAST)

    def prepare(k):
        lane = lax.broadcasted_iota(jnp.int32, (rows, HD), 1)
        lses = lse_ref[0].T * ROOT
        heads = lax.broadcasted_iota(jnp.int32, lses.shape, 1)

        def one(h, _):
            lanes = pl.ds(pl.multiple_of(h * HD, HD), HD)
            prod = do_ref[:, lanes].astype(F32) * o_ref[:, lanes].astype(F32)
            delta = jnp.sum(prod, axis=1, keepdims=True)
            lse = jnp.sum(jnp.where(heads == h, lses, 0.0), axis=1, keepdims=True)
            w = jnp.where(lane == 3, 1.0, 0.0)
            for i, x in enumerate(split3(lse)):
                w = jnp.where(lane == i, x, w)
            for i, x in enumerate(split3(delta)):
                w = jnp.where(lane == 4 + i, x, w)
            aug[h] = w.astype(BF)
            return 0

        lax.fori_loop(k * GROUP, (k + 1) * GROUP, one, 0)
        if k > 0:
            return
        vcon[...] = jnp.where(both(lane >= 4, lane < 7), -1.0, 0.0).astype(BF)
        mine = layout[2 * b + p // 2]
        for role, owner in enumerate((b, d_from, blk(sib - 2), behind)):
            for s in range(2):
                bias = jnp.where(layout[2 * owner + s] > mine, -BIG, 0.0)
                w = jnp.where(lane == 3, bias, jnp.where(lane < 3, -1.0, 0.0)).astype(BF)
                kcon[role, 2 * s] = w
                kcon[role, 2 * s + 1] = w

    keys_n = LINE * rows

    def chunk(k, role, own):
        keys = got[role, k, :, 0].reshape(keys_n, HD)
        vals = got[role, k, :, 1].reshape(keys_n, HD)
        ka = jnp.concatenate([keys, kcon[role].reshape(keys_n, HD)], axis=1)
        va = jnp.concatenate([vals, jnp.concatenate([vcon[...]] * LINE, axis=0)], axis=1)
        qs, gs, qa, ga = [], [], [], []
        for g in range(GROUP):
            h = k * GROUP + g
            lanes = pl.ds(pl.multiple_of(h * HD, HD), HD)
            qs.append(q_ref[:, lanes])
            gs.append(do_ref[:, lanes])
            w = aug[h]
            qa.append(jnp.concatenate([qs[-1], w], axis=1))
            ga.append(jnp.concatenate([gs[-1], w], axis=1))
        qs, gs, qa, ga = [jnp.concatenate(x, axis=0) for x in (qs, gs, qa, ga)]
        st = nt(ka, qa)
        if own:
            j = lax.broadcasted_iota(jnp.int32, st.shape, 0)
            t = lax.rem(lax.broadcasted_iota(jnp.int32, st.shape, 1), rows) + p * rows
            half = 2 * rows
            low = (p // 2) * half
            hidden = both(j > t, j >= low, j < low + half)
            st = jnp.where(hidden, -BIG, st)
        prob = jnp.exp2(st * EXP2_SCALE)
        ds = (prob * nt(va, ga)).astype(BF)
        part[role, k, :, 1] = nn(prob.astype(BF), gs).reshape(LINE, rows, HD).astype(BF)
        part[role, k, :, 0] = nn(ds, qs).reshape(LINE, rows, HD).astype(BF)
        kept[k, role] = ds

    def dq_copy(k):
        lanes = pl.ds(pl.multiple_of(k * GROUP * HD, GROUP * HD), GROUP * HD)
        return pltpu.make_async_copy(dq_ref.at[:, lanes], dq_hbm.at[0, :, lanes], sem_out.at[k])

    def dq_out(k):
        keys = got[:, k, :, 0].reshape(4 * keys_n, HD)
        total = tn(keys, kept[k].reshape(4 * keys_n, GROUP * rows)) * (2 * SCALE)
        for g in range(GROUP):
            lanes = pl.ds(pl.multiple_of((k * GROUP + g) * HD, HD), HD)
            dq_ref[:, lanes] = total[:, g * rows:(g + 1) * rows].T.astype(BF)
        dq_copy(k).start()

    loads = [
        pltpu.make_async_copy(src.at[0], dst, sem_in.at[i])
        for i, (src, dst) in enumerate(((do_hbm, do_ref), (o_hbm, o_ref), (q_hbm, q_ref)))
    ]
    for k in range(KVH):
        own_copy(k, 0).start()
        own_copy(k, 1).start()
    for load in loads:
        load.start()

    barrier = pltpu.get_barrier_semaphore()

    def greet(dev):
        pl.semaphore_signal(barrier, inc=1, device_id=dev, device_id_type=MESH)

    greet(at(sib, p))
    greet(at(blk(b + 3 - 6 * (1 - core)), p))
    for away in range(1, LINE):
        greet(at(b, lax.rem(p + away, LINE)))
    at_end = jnp.logical_or(p == 0, p == LINE - 1)

    @pl.when(at_end)
    def _():
        greet(at(ahead, 3 - p))
        greet(at(behind, 3 - p))

    pl.semaphore_wait(barrier, jnp.where(at_end, 7, 5))

    own_send(0)
    own_send(1)
    loads[0].wait()
    loads[1].wait()
    prepare(0)
    gather(0, 0)
    own_send(2)
    prepare(1)
    gather(0, 1)
    gather(1, 0)
    own_send(3)
    prepare(2)
    prepare(3)
    gather(0, 2)
    gather(1, 1)
    gather(2, 0)
    c_d_all(0).start()
    loads[2].wait()

    def when(cond, f):
        pl.when(cond)(f)

    def step(c, _):
        wave = lax.div(c + 5, 2)
        for j in (3, 2, 1, 0):
            k = wave - j
            when(both(lax.rem(c, 2) == 1, k >= 0, k < KVH), lambda j=j, k=k: gather(k, j))
        when(both(c > 0, c < 7, lax.rem(c, 2) == 0), lambda: c_d_all(lax.div(c, 2)).start())

        def pick(*pairs):
            out = pairs[-1]
            for cond, value in reversed(pairs[:-1]):
                out = jnp.where(cond, value, out)
            return out

        for t, gaps in enumerate(((5, 9, 13, 15), (9, 11, 14), (11, 13), (13, 15), (15,))):
            k = pick(*((c == gap, k) for k, gap in enumerate(gaps)), -1)
            when(k >= 0, lambda t=t, k=k: back(k, t))

        i = pick((c >= 13, 3), (c >= 11, 2), (c == 10, 3), (c == 9, 2), (c >= 6, 1), (c == 5, 2), (c == 1, 1), 0)
        role = pick(
            (c == 15, 0), (c >= 11, 2 + lax.rem(c + 1, 2)), (c >= 9, 1), (c >= 6, lax.rem(c, 3) + 1),
            (c == 4, 1), (jnp.logical_or(c == 2, c == 3), c), 0,
        )
        when(role == 1, lambda: c_d_all(i).wait_recv())
        when(role == 2, lambda: c_sib_all(i).wait_recv())
        when(role == 0, lambda: chunk(i, 0, True))
        when(role > 0, lambda: chunk(i, role, False))
        when(role == 1, lambda: r_d(i).start())
        when(role == 2, lambda: r_sib(i).start())
        return 0

    lax.fori_loop(0, 4 * KVH, step, 0)
    back_last(1)
    back(2, 2)

    def queries_back(k, _):
        dq_out(k)
        return 0

    lax.fori_loop(0, 2, queries_back, 0)
    back(1, 4)
    back_last(2)
    back(2, 3)
    lax.fori_loop(2, KVH, queries_back, 0)
    back_last(3)
    back(2, 4)

    def drain(k, _):
        for u in range(LINE):
            spread(k, u, wait_send)
            pass_on(k, u, wait_send)
            send_back(k, u, wait_send)
            pl.when(u != p)(lambda: r_left(k, u).wait_send())
        c_d_all(k).wait_send()
        c_sib_all(k).wait_send()
        r_d(k).wait_send()
        r_sib(k).wait_send()
        return 0

    lax.fori_loop(0, KVH, drain, 0)
    for k in range(KVH):
        dq_copy(k).wait()


def solution(mesh):
    n = mesh.shape["blk"]
    vm = pl.BlockSpec(memory_space=pltpu.VMEM)
    anywhere = pl.BlockSpec(memory_space=pl.ANY)

    def shards(queries, key_rows, value_rows, attn_out, out_grad, log_norm, block_layout):
        rows = queries.shape[1]
        unit = (KVH, LINE, 2, rows, HD)
        sem = pltpu.SemaphoreType.DMA((KVH, LINE))
        sems = pltpu.SemaphoreType.DMA((KVH,))
        log_norm = jnp.transpose(log_norm, (0, 2, 1))
        twice = pl.pallas_call(
            functools.partial(kernel, n),
            out_shape=(
                jax.ShapeDtypeStruct(queries.shape, BF),
                jax.ShapeDtypeStruct(key_rows.shape, BF),
                jax.ShapeDtypeStruct(value_rows.shape, BF),
            ),
            in_specs=[
                pl.BlockSpec(memory_space=pltpu.SMEM),
            ] + [anywhere] * 5 + [
                vm,
            ],
            out_specs=(anywhere, vm, vm),
            scratch_shapes=[
                pltpu.VMEM(queries.shape[1:], BF),
                pltpu.VMEM(queries.shape[1:], BF),
                pltpu.VMEM(queries.shape[1:], BF),
                pltpu.VMEM(queries.shape[1:], BF),
                pltpu.SemaphoreType.DMA((3,)),
                sems,
                pltpu.VMEM((4,) + unit, BF),
                pltpu.VMEM((KVH * GROUP, rows, HD), BF),
                pltpu.VMEM((4, LINE, rows, HD), BF),
                pltpu.VMEM((rows, HD), BF),
                pltpu.VMEM((KVH, 4, LINE * rows, GROUP * rows), BF),
                pltpu.VMEM((4,) + unit, BF),
                pltpu.VMEM((2, rows, HD), F32),
            ]
            + [pltpu.VMEM(unit, BF)] * 8
            + [pltpu.VMEM((LINE, 2, rows, HD), BF)]
            + [pltpu.SemaphoreType.DMA((KVH, 2))]
            + [sem] * 4 + [sems] * 2 + [sem] * 2 + [sems] * 2
            + [sem] * 2 + [sems] * 2 + [sem] * 4 + [sems] * 3,
            compiler_params=pltpu.CompilerParams(
                collective_id=0, has_side_effects=True, vmem_limit_bytes=56 * 2**20
            ),
        )(block_layout, queries, key_rows, value_rows, attn_out, out_grad, log_norm)
        return tuple(x * jnp.asarray(0.5, BF) for x in twice)

    placed = P("blk", "head", None)
    return jax.shard_map(
        shards,
        mesh=mesh,
        in_specs=(placed,) * 6 + (P(),),
        out_specs=(placed,) * 3,
        check_vma=False,
    )
```

```python
import functools
import math

import jax
import jax.numpy as jnp
from jax import lax
from jax.experimental import pallas as pl
from jax.experimental.pallas import tpu as pltpu
from jax.sharding import PartitionSpec as P

HD = 128
GROUP = 8
KVH = 4
ROOT = math.sqrt(HD)
SCALE = 1.0 / ROOT
EXP2_SCALE = math.log2(math.e) / ROOT
BIG = 1e30
LINE = 4
REACH = (0, 1, 3, 4)
REACH_LAST = (1, 2, 2, 3)
LAST = KVH - 1
ORDER = (
    (0, 0), (1, 0), (2, 0), (0, 2), (0, 3), (0, 1), (1, 2), (1, 3),
    (1, 1), (2, 1), (2, 2), (2, 3), (3, 1), (3, 2), (3, 3), (3, 0),
)
BACK_GAPS = ((5, 8, 12, 15), (10, 13, 15), (12, 15), (14,), ())
MESH = pl.DeviceIdType.MESH
BF = jnp.bfloat16
F32 = jnp.float32


def nt(a, b):
    return lax.dot_general(a, b, (((1,), (1,)), ((), ())), preferred_element_type=F32)


def nn(a, b):
    return lax.dot_general(a, b, (((1,), (0,)), ((), ())), preferred_element_type=F32)


def tn(a, b):
    return lax.dot_general(a, b, (((0,), (0,)), ((), ())), preferred_element_type=F32)


def split3(x):
    hi = x.astype(BF).astype(F32)
    mid = (x - hi).astype(BF).astype(F32)
    return hi, mid, x - hi - mid


def kernel(
    n, layout, q_hbm, k_hbm, v_hbm, o_hbm, do_hbm, lse_ref,
    dq_hbm, dk_ref, dv_ref,
    q_ref, o_ref, do_ref, dq_ref, sem_in, sem_out, got, aug, kcon, vcon, kept, part, acc, out_c, out_l,
    in_s, in_d, in_c, in_x, in_r, in_w, in_u,
    sem_own, s_r, s_w, s_x, s_c, s_d, s_s, g_l, g_c, g_d, g_s,
    t_c, t_l, t_s, t_d, h_c, h_x, h_r, h_w, h_s, h_d, h_u,
):
    rows = q_ref.shape[0]
    b = lax.axis_index("blk")
    p = lax.axis_index("head")
    core = lax.rem(b, 2)
    lbuf, dbuf, sbuf, cbuf = [got.at[role] for role in range(4)]

    def blk(i):
        return lax.rem(i + n, n)

    sib = b + 1 - 2 * core
    d_to = blk(b + 1 + 2 * core)
    d_from = blk(b - 3 + 2 * core)
    ahead = blk(b + 2)
    behind = blk(b - 2)

    def at(bb, pp):
        return {"blk": bb, "head": pp}

    def both(*conds):
        out = conds[0]
        for c in conds[1:]:
            out = jnp.logical_and(out, c)
        return out

    def reach(u, k):
        if isinstance(k, int):
            return REACH_LAST[u] if k % 2 == 1 else REACH[u]
        return jnp.where(lax.rem(k, 2) == 1, REACH_LAST[u], REACH[u])

    def copy(src, dst, send, recv, dev):
        return pltpu.make_async_remote_copy(
            src_ref=src, dst_ref=dst, send_sem=send, recv_sem=recv,
            device_id=dev, device_id_type=MESH,
        )

    def c_right(k, u):
        return copy(lbuf.at[k, u], lbuf.at[k, u], s_r.at[k, u], g_l.at[k, u], at(b, p + 1))

    def c_left(k, u):
        return copy(lbuf.at[k, u], lbuf.at[k, u], s_w.at[k, u], g_l.at[k, u], at(b, p - 1))

    def c_cross(k, u):
        return copy(lbuf.at[k, u], cbuf.at[k, u], s_x.at[k, u], g_c.at[k, u], at(ahead, 3 - p))

    def c_on(k, u, step):
        return copy(cbuf.at[k, u], cbuf.at[k, u], s_c.at[k, u], g_c.at[k, u], at(b, p + step))

    def c_sib(k, u):
        return copy(cbuf.at[k, u], sbuf.at[k, u], s_s.at[k], g_s.at[k], at(sib, p))

    def c_d_all(k):
        return copy(lbuf.at[k], dbuf.at[k], s_d.at[k], g_d.at[k], at(d_to, p))

    def c_sib_all(k):
        return copy(cbuf.at[k], sbuf.at[k], s_s.at[k], g_s.at[k], at(sib, p))

    def r_sib(k):
        return copy(part.at[2, k], in_s.at[k], t_s.at[k], h_s.at[k], at(sib, p))

    def r_d(k):
        return copy(part.at[1, k], in_d.at[k], t_d.at[k], h_d.at[k], at(d_from, p))

    def r_back(k, u, step):
        return copy(out_c.at[k, u], in_c.at[k, u], t_c.at[k, u], h_c.at[k, u], at(b, p + step))

    def r_cross(k, u):
        return copy(out_c.at[k, u], in_x.at[k, u], t_c.at[k, u], h_x.at[k, u], at(behind, 3 - p))

    def r_left(k, u):
        return copy(out_l.at[k, u], in_r.at[k, u], t_l.at[k, u], h_r.at[k, u], at(b, p - 1))

    def r_right(k, u):
        return copy(out_l.at[k, u], in_w.at[k, u], t_l.at[k, u], h_w.at[k, u], at(b, p + 1))

    def r_owner(u, place):
        return copy(out_l.at[LAST, u], in_u.at[place], t_l.at[LAST, u], h_u.at[place], at(b, u))

    start = lambda c: c.start()
    wait_send = lambda c: c.wait_send()

    def crosses(k, u):
        return jnp.logical_or(
            both(p == LINE - 1, reach(u, k) > 0), both(p == 0, reach(u, k) < LINE)
        )

    def spread(k, u, act):
        pl.when(crosses(k, u))(lambda: act(c_cross(k, u)))
        pl.when(both(u <= p, p < LINE - 1))(lambda: act(c_right(k, u)))
        pl.when(both(u >= p, p > 0))(lambda: act(c_left(k, u)))

    def pass_on(k, u, act):
        top = reach(u, k)
        pl.when(p + 1 < top)(lambda: act(c_on(k, u, 1)))
        pl.when(p > top)(lambda: act(c_on(k, u, -1)))

    def own_copy(k, which):
        src = (k_hbm, v_hbm)[which]
        lanes = pl.ds(pl.multiple_of(k * HD, HD), HD)
        return pltpu.make_async_copy(
            src.at[0, :, lanes], lbuf.at[k, p, which], sem_own.at[k, which]
        )

    def own_send(k):
        own_copy(k, 0).wait()
        own_copy(k, 1).wait()
        for u in range(LINE):
            @pl.when(p == u)
            def _(u=u):
                spread(k, u, start)

    def gather(k, j):
        for u in range(LINE):
            if j < LINE - 1:
                @pl.when(jnp.logical_or(p - u == j + 1, u - p == j + 1))
                def _(u=u):
                    c_right(k, u).wait_recv()
                    spread(k, u, start)

            top = reach(u, k)
            rise = both(p < top, p + (3 - u) == j)
            fall = both(p >= top, u + 3 - p == j)

            @pl.when(jnp.logical_or(rise, fall))
            def _(u=u):
                c_cross(k, u).wait_recv()
                pass_on(k, u, start)
                c_sib(k, u).start()

    def add(src, k, u):
        acc[...] += src[k, u].astype(F32)

    def send_back(k, u, act):
        top = reach(u, k)
        pl.when(both(p < top, p > 0))(lambda: act(r_back(k, u, -1)))
        pl.when(both(p >= top, p < LINE - 1))(lambda: act(r_back(k, u, 1)))
        pl.when(jnp.logical_or(both(p < top, p == 0), both(p >= top, p == LINE - 1)))(
            lambda: act(r_cross(k, u))
        )

    def line_terms(k, u):
        acc[...] = part[0, k, u].astype(F32)
        add(in_d, k, u)

        @pl.when(crosses(k, u))
        def _():
            r_cross(k, u).wait_recv()
            add(in_x, k, u)

    def from_right(k, u):
        r_left(k, u).wait_recv()
        add(in_r, k, u)

    def from_left(k, u):
        r_right(k, u).wait_recv()
        add(in_w, k, u)

    def finish(k, u):
        line_terms(k, u)
        pl.when(p < LINE - 1)(lambda: from_right(k, u))
        pl.when(p > 0)(lambda: from_left(k, u))
        write_out(k)

    def write_out(k):
        lanes = pl.ds(pl.multiple_of(k * HD, HD), HD)
        dk_ref[0, :, lanes] = (acc[0] * (2 * SCALE)).astype(BF)
        dv_ref[0, :, lanes] = (acc[1] * 2.0).astype(BF)

    def line_ahead(k, t):
        for u in range(LINE):
            top = reach(u, k)

            @pl.when(jnp.logical_or(p == top - 1 - t, p == top + t))
            def _(u=u):
                acc[...] = part[3, k, u].astype(F32)
                add(in_s, k, u)
                if t > 0:
                    r_back(k, u, 0).wait_recv()
                    add(in_c, k, u)
                out_c[k, u] = acc[...].astype(BF)
                send_back(k, u, start)

    def back(k, t):
        if t == 0:
            r_sib(k).wait_recv()
        if t == 1:
            r_d(k).wait_recv()
        if t < LINE:
            line_ahead(k, t)
        for u in range(LINE):
            top = reach(u, k)
            if t > 0:
                @pl.when(both(p > u, jnp.maximum(1, top) + 3 - p == t))
                def _(u=u):
                    line_terms(k, u)
                    pl.when(p < LINE - 1)(lambda: from_right(k, u))
                    out_l[k, u] = acc[...].astype(BF)
                    r_left(k, u).start()

                @pl.when(both(p < u, jnp.maximum(1, LINE - top) + p == t))
                def _(u=u):
                    line_terms(k, u)
                    pl.when(p > 0)(lambda: from_left(k, u))
                    out_l[k, u] = acc[...].astype(BF)
                    r_right(k, u).start()

            if t == LINE:
                pl.when(p == u)(lambda u=u: finish(k, u))

    def back_last(t):
        if t == 1:
            r_d(LAST).wait_recv()
        if t < LINE - 1:
            line_ahead(LAST, t)
        for u in range(LINE):
            top = REACH_LAST[u]
            turn = jnp.where(p == LINE - 1, max(1, top), jnp.where(p == 0, max(1, LINE - top), 1))

            @pl.when(both(p != u, turn == t))
            def _(u=u):
                line_terms(LAST, u)
                out_l[LAST, u] = acc[...].astype(BF)
                r_owner(u, p).start()

        if t == LINE - 1:
            for u in range(LINE):
                @pl.when(p == u)
                def _(u=u):
                    line_terms(LAST, u)
                    for place in range(LINE):
                        if place != u:
                            r_owner((u + 1) % LINE, place).wait_recv()
                            acc[...] += in_u[place].astype(F32)
                    write_out(LAST)

    def prepare(k):
        lane = lax.broadcasted_iota(jnp.int32, (rows, HD), 1)
        lses = lse_ref[0].T * ROOT
        heads = lax.broadcasted_iota(jnp.int32, lses.shape, 1)

        def one(h, _):
            lanes = pl.ds(pl.multiple_of(h * HD, HD), HD)
            prod = do_ref[:, lanes].astype(F32) * o_ref[:, lanes].astype(F32)
            delta = jnp.sum(prod, axis=1, keepdims=True)
            lse = jnp.sum(jnp.where(heads == h, lses, 0.0), axis=1, keepdims=True)
            w = jnp.where(lane == 3, 1.0, 0.0)
            for i, x in enumerate(split3(lse)):
                w = jnp.where(lane == i, x, w)
            for i, x in enumerate(split3(delta)):
                w = jnp.where(lane == 4 + i, x, w)
            aug[h] = w.astype(BF)
            return 0

        lax.fori_loop(k * GROUP, (k + 1) * GROUP, one, 0)
        if k > 0:
            return
        vcon[...] = jnp.where(both(lane >= 4, lane < 7), -1.0, 0.0).astype(BF)
        mine = layout[2 * b + p // 2]
        for role, owner in enumerate((b, d_from, blk(sib - 2), behind)):
            for s in range(2):
                bias = jnp.where(layout[2 * owner + s] > mine, -BIG, 0.0)
                w = jnp.where(lane == 3, bias, jnp.where(lane < 3, -1.0, 0.0)).astype(BF)
                kcon[role, 2 * s] = w
                kcon[role, 2 * s + 1] = w

    keys_n = LINE * rows

    def chunk(k, role, own):
        keys = got[role, k, :, 0].reshape(keys_n, HD)
        vals = got[role, k, :, 1].reshape(keys_n, HD)
        ka = jnp.concatenate([keys, kcon[role].reshape(keys_n, HD)], axis=1)
        va = jnp.concatenate([vals, jnp.concatenate([vcon[...]] * LINE, axis=0)], axis=1)
        qs, gs, qa, ga = [], [], [], []
        for g in range(GROUP):
            h = k * GROUP + g
            lanes = pl.ds(pl.multiple_of(h * HD, HD), HD)
            qs.append(q_ref[:, lanes])
            gs.append(do_ref[:, lanes])
            w = aug[h]
            qa.append(jnp.concatenate([qs[-1], w], axis=1))
            ga.append(jnp.concatenate([gs[-1], w], axis=1))
        qs, gs, qa, ga = [jnp.concatenate(x, axis=0) for x in (qs, gs, qa, ga)]
        st = nt(ka, qa)
        if own:
            j = lax.broadcasted_iota(jnp.int32, st.shape, 0)
            t = lax.rem(lax.broadcasted_iota(jnp.int32, st.shape, 1), rows) + p * rows
            half = 2 * rows
            low = (p // 2) * half
            hidden = both(j > t, j >= low, j < low + half)
            st = jnp.where(hidden, -BIG, st)
        prob = jnp.exp2(st * EXP2_SCALE)
        ds = (prob * nt(va, ga)).astype(BF)
        part[role, k, :, 1] = nn(prob.astype(BF), gs).reshape(LINE, rows, HD).astype(BF)
        part[role, k, :, 0] = nn(ds, qs).reshape(LINE, rows, HD).astype(BF)
        kept[k, role] = ds

    def dq_copy(k):
        lanes = pl.ds(pl.multiple_of(k * GROUP * HD, GROUP * HD), GROUP * HD)
        return pltpu.make_async_copy(dq_ref.at[:, lanes], dq_hbm.at[0, :, lanes], sem_out.at[k])

    def dq_out(k):
        keys = got[:, k, :, 0].reshape(4 * keys_n, HD)
        total = tn(keys, kept[k].reshape(4 * keys_n, GROUP * rows)) * (2 * SCALE)
        for g in range(GROUP):
            lanes = pl.ds(pl.multiple_of((k * GROUP + g) * HD, HD), HD)
            dq_ref[:, lanes] = total[:, g * rows:(g + 1) * rows].T.astype(BF)
        dq_copy(k).start()

    loads = [
        pltpu.make_async_copy(src.at[0], dst, sem_in.at[i])
        for i, (src, dst) in enumerate(((do_hbm, do_ref), (o_hbm, o_ref), (q_hbm, q_ref)))
    ]
    for k in range(KVH):
        own_copy(k, 0).start()
        own_copy(k, 1).start()
    for load in loads:
        load.start()

    barrier = pltpu.get_barrier_semaphore()

    def greet(dev):
        pl.semaphore_signal(barrier, inc=1, device_id=dev, device_id_type=MESH)

    greet(at(sib, p))
    greet(at(blk(b + 3 - 6 * (1 - core)), p))
    for away in range(1, LINE):
        greet(at(b, lax.rem(p + away, LINE)))
    at_end = jnp.logical_or(p == 0, p == LINE - 1)

    @pl.when(at_end)
    def _():
        greet(at(ahead, 3 - p))
        greet(at(behind, 3 - p))

    pl.semaphore_wait(barrier, jnp.where(at_end, 7, 5))

    own_send(0)
    own_send(1)
    loads[0].wait()
    loads[1].wait()
    prepare(0)
    gather(0, 0)
    own_send(2)
    prepare(1)
    gather(1, 0)
    own_send(3)
    gather(0, 1)
    gather(2, 0)
    prepare(2)
    gather(1, 1)
    gather(3, 0)
    prepare(3)
    gather(0, 2)
    gather(2, 1)
    loads[2].wait()

    def when(cond, f):
        pl.when(cond)(f)

    def step(c, _):
        for j in (3, 2, 1):
            k = c + 4 - 2 * j
            when(both(c > 0, k >= 0, k < KVH), lambda j=j, k=k: gather(k, j))
        when(c == 1, lambda: c_d_all(0).start())
        when(both(c >= 3, c <= 5), lambda: c_d_all(c - 2).start())

        def pick(*pairs):
            out = pairs[-1]
            for cond, value in reversed(pairs[:-1]):
                out = jnp.where(cond, value, out)
            return out

        for t, gaps in enumerate(BACK_GAPS):
            k = pick(*((c == gap, k) for k, gap in enumerate(gaps)), -1)
            when(k >= 0, lambda t=t, k=k: back(k, t))

        def table(entries):
            return pick(*((c == at_c, v) for at_c, v in enumerate(entries)), entries[-1])

        i = table([k for k, _ in ORDER])
        role = table([r for _, r in ORDER])
        when(role == 1, lambda: c_d_all(i).wait_recv())
        when(role == 2, lambda: c_sib_all(i).wait_recv())
        when(role == 0, lambda: chunk(i, 0, True))
        when(role > 0, lambda: chunk(i, role, False))
        when(role == 1, lambda: r_d(i).start())
        when(role == 2, lambda: r_sib(i).start())
        return 0

    lax.fori_loop(0, 4 * KVH, step, 0)
    def queries_back(k, _):
        dq_out(k)
        return 0

    back(0, 4)
    back_last(1)
    back(1, 3)
    back(2, 2)
    lax.fori_loop(0, 2, queries_back, 0)
    back(1, 4)
    back_last(2)
    back(2, 3)
    lax.fori_loop(2, 4, queries_back, 0)
    back_last(3)
    back(2, 4)

    def drain(k, _):
        for u in range(LINE):
            spread(k, u, wait_send)
            pass_on(k, u, wait_send)
            send_back(k, u, wait_send)
            pl.when(u != p)(lambda: r_left(k, u).wait_send())
        c_d_all(k).wait_send()
        c_sib_all(k).wait_send()
        r_d(k).wait_send()
        r_sib(k).wait_send()
        return 0

    lax.fori_loop(0, KVH, drain, 0)
    for k in range(KVH):
        dq_copy(k).wait()


def solution(mesh):
    n = mesh.shape["blk"]
    vm = pl.BlockSpec(memory_space=pltpu.VMEM)
    anywhere = pl.BlockSpec(memory_space=pl.ANY)

    def shards(queries, key_rows, value_rows, attn_out, out_grad, log_norm, block_layout):
        rows = queries.shape[1]
        unit = (KVH, LINE, 2, rows, HD)
        sem = pltpu.SemaphoreType.DMA((KVH, LINE))
        sems = pltpu.SemaphoreType.DMA((KVH,))
        log_norm = jnp.transpose(log_norm, (0, 2, 1))
        twice = pl.pallas_call(
            functools.partial(kernel, n),
            out_shape=(
                jax.ShapeDtypeStruct(queries.shape, BF),
                jax.ShapeDtypeStruct(key_rows.shape, BF),
                jax.ShapeDtypeStruct(value_rows.shape, BF),
            ),
            in_specs=[
                pl.BlockSpec(memory_space=pltpu.SMEM),
            ] + [anywhere] * 5 + [
                vm,
            ],
            out_specs=(anywhere, vm, vm),
            scratch_shapes=[
                pltpu.VMEM(queries.shape[1:], BF),
                pltpu.VMEM(queries.shape[1:], BF),
                pltpu.VMEM(queries.shape[1:], BF),
                pltpu.VMEM(queries.shape[1:], BF),
                pltpu.SemaphoreType.DMA((3,)),
                sems,
                pltpu.VMEM((4,) + unit, BF),
                pltpu.VMEM((KVH * GROUP, rows, HD), BF),
                pltpu.VMEM((4, LINE, rows, HD), BF),
                pltpu.VMEM((rows, HD), BF),
                pltpu.VMEM((KVH, 4, LINE * rows, GROUP * rows), BF),
                pltpu.VMEM((4,) + unit, BF),
                pltpu.VMEM((2, rows, HD), F32),
            ]
            + [pltpu.VMEM(unit, BF)] * 8
            + [pltpu.VMEM((LINE, 2, rows, HD), BF)]
            + [pltpu.SemaphoreType.DMA((KVH, 2))]
            + [sem] * 4 + [sems] * 2 + [sem] * 2 + [sems] * 2
            + [sem] * 2 + [sems] * 2 + [sem] * 4 + [sems] * 3,
            compiler_params=pltpu.CompilerParams(
                collective_id=0, has_side_effects=True, vmem_limit_bytes=56 * 2**20
            ),
        )(block_layout, queries, key_rows, value_rows, attn_out, out_grad, log_norm)
        return tuple(x * jnp.asarray(0.5, BF) for x in twice)

    placed = P("blk", "head", None)
    return jax.shard_map(
        shards,
        mesh=mesh,
        in_specs=(placed,) * 6 + (P(),),
        out_specs=(placed,) * 3,
        check_vma=False,
    )
```
